256 devices in a mesh: expert: 32 (over y, z_hi, core), dp: 8 (over x, z_lo).
Axes of the slice: x: 4, y: 4, z: 8 (z_hi: 4, z_lo: 2; z = z_hi * 2 + z_lo), core: 2. Of those that a mesh axis runs over, the one named last changes fastest.
Arguments:
- tokens: bfloat16 [12288, 4096], P(('expert', 'dp')), may hold values from -6 to 6
- cotangent: bfloat16 [12288, 4096], P(('expert', 'dp')), may hold values from -6 to 6
- expert_ids: int32 [12288, 8], P(('expert', 'dp')), may hold values from 0 to 31, all different within a row; in each aligned block of 48 rows (0 to 47, 48 to 95, ...) at most 13 rows name the same one
- gate_values: float32 [12288, 8], P(('expert', 'dp')), may hold values from 0.03 to 0.3
- expert_home: int32 [32], replicated, may hold values from 0 to 31, each once
- swap_flag: int32 [16], replicated, may hold values from 0 to 1, as said below
- weight_in: bfloat16 [32, 4096, 768], P('expert', 'dp'), may hold values from -0.09375 to 0.09375
- weight_out: bfloat16 [32, 768, 4096], P('expert', None, 'dp'), may hold values from -0.21875 to 0.21875
Outputs:
- grad_tokens: bfloat16 [12288, 4096], P(('expert', 'dp'))
- weight_in_grad: bfloat16 [32, 4096, 768], P('expert', 'dp')
- weight_out_grad: bfloat16 [32, 768, 4096], P('expert', None, 'dp')
The draws below stay inside these ranges and needn't reach their ends.
Inputs may be any that keep to these rules, and one draw needn't show every extreme that they name: `expert_ids`: each row names 8 different experts; among the rows of one device no expert is named more than 13 times. `expert_home`: each expert once. `swap_flag`: the last pair always swaps.
All inputs are finite; a program needn't handle non-finite values.
Results may differ from the reference program's by a relative error of at most 0.017.
Values may be sent and summed in bfloat16 or wider, within the bound.
No kernel may reach another device: no remote copies, remote signals or barrier semaphores. Data moves between devices by JAX's collectives and lax.ppermute only.
A program may use at most 128 MiB of HBM per device.

```python
import math
import jax
import jax.numpy as jnp
import numpy as np
from jax import lax

D = 4096
F = 768
TOP = 8
TOK_DEV = 48
EXPERTS = 32
CAP = 13
TOKENS = 12288
N_EXPERT = 32
N_DP = 8


def draw_swap_flag(key, part):
    key = jax.random.fold_in(key, 5)
    pairs = EXPERTS // 2
    coins = jax.random.randint(key, (pairs,), 0, 2, dtype=jnp.int32)
    return jnp.where(jnp.arange(pairs) == pairs - 1, 1, coins).astype(jnp.int32)


def level_of(key, shape, cuts, least, largest):
    def one(axis_at, blocks):
        steps = jax.random.uniform(jax.random.fold_in(jax.random.fold_in(key, 6), axis_at), (blocks,), jnp.float32, least / len(cuts), largest / len(cuts))
        return jnp.repeat(jnp.exp(steps), shape[axis_at] // blocks).reshape((-1,) + (1,) * (len(shape) - axis_at - 1))

    factor_of = one(*cuts[0])
    for cut in cuts[1:]:
        factor_of = factor_of * one(*cut)
    return factor_of


def routed_block(stream_key, own, number, rows, number_of, top, bound, skew):
    ranking = jax.random.permutation(stream_key, number_of)
    packed, common = load_shares(number_of, rows * top, bound, skew, True), load_shares(number_of, rows * top, bound, skew, False)
    places = jnp.arange(number_of)

    def named(tallies, offset_by):
        used = int((tallies > 0).sum())
        fixed = max(1, used // 4)
        shifted = fixed + (places - fixed + offset_by * (used - fixed)) % max(1, number_of - fixed)
        return jnp.zeros((number_of,), jnp.int32).at[ranking[jnp.where(places < fixed, places, shifted)]].set(jnp.asarray(tallies, jnp.int32))

    tallies = jnp.where(number % 4 == 0, named(packed, number // 4), named(common, number - number // 4 - 1))
    mixed = jax.random.permutation(jax.random.fold_in(own, 3), number_of)
    source_of, receiver = mixed[0:number_of // 2 * 2:2], mixed[1:number_of // 2 * 2:2]
    room = jnp.minimum(tallies[source_of] - 1, bound - tallies[receiver]) // 2
    room = jnp.where((source_of == ranking[0]) | (receiver == ranking[0]) | (tallies[receiver] == 0), 0, jnp.maximum(room, 0))
    shifted = jax.random.randint(jax.random.fold_in(own, 4), (number_of // 2,), 0, 1 << 20) % (room + 1)
    tallies = tallies.at[source_of].add(-shifted).at[receiver].add(shifted)
    labels = jnp.searchsorted(jnp.cumsum(tallies), jnp.arange(rows * top), side="right").astype(jnp.int32)
    listing = labels.reshape(top, rows).T
    listing = listing[jax.random.permutation(jax.random.fold_in(own, 1), rows)]
    offset_by = jax.random.randint(jax.random.fold_in(own, 2), (rows, 1), 0, top)
    return jnp.take_along_axis(listing, (jnp.arange(top)[None, :] + offset_by) % top, axis=1)


def load_shares(number_of, total, reach, lean, full):
    weights = [(1 << 20) // math.isqrt(grade ** lean) + 1 for grade in range(1, number_of + 1)]
    largest = reach if full else min(reach, max(-(-total // number_of), total * weights[0] // sum(weights)))
    least = 1 if total - largest >= number_of - 1 else 0
    given, spare = [largest] + [least] * (number_of - 1), total - largest - least * (number_of - 1)
    while spare > 0:
        candidates = [i for i in range(1, number_of) if given[i] < largest] or [i for i in range(1, number_of) if given[i] < reach]
        whole, budget = sum([weights[i] for i in candidates]), spare
        for i in candidates:
            addition = min(reach - given[i], max(1, budget * weights[i] // whole), spare)
            given[i] = given[i] + addition
            spare = spare - addition
    return np.array(given)


def gaussian(stream_key, shape, deviation, most, shards=(), kind=jnp.bfloat16):
    gain = level_of(stream_key, shape, shards, -0.22, 0.18) if shards else 1.0
    values = jax.random.normal(stream_key, shape, jnp.float32) * deviation * gain
    return jnp.minimum(jnp.maximum(values, -most), most).astype(kind)


def setup_inputs(seed: int = 0) -> dict:
    key_of = jax.random.split(jax.random.key(seed), 9)
    tokens = gaussian(key_of[0], (TOKENS, D), 1.0, 6.0, ((0, 256),))
    cotangent = gaussian(key_of[1], (TOKENS, D), 1.0, 6.0, ((0, 256),))
    expert_ids_keys = jax.random.split(jax.random.fold_in(key_of[2], 1), TOKENS // TOK_DEV)
    expert_ids_turns = jax.random.permutation(jax.random.fold_in(key_of[2], 3), TOKENS // TOK_DEV)
    expert_ids = jax.vmap(lambda own, number: routed_block(jax.random.fold_in(key_of[2], 2), own, number, TOK_DEV, EXPERTS, TOP, CAP, 1))(expert_ids_keys, expert_ids_turns).reshape((TOKENS, TOP))
    gate_values = jnp.clip(jnp.exp(math.log(0.3) - 2.3025852 * jax.random.uniform(key_of[3], (TOKENS, TOP), jnp.float32) ** level_of(key_of[3], (TOKENS, TOP), ((0, 256),), -0.2, 0.2)), 0.03, 0.3)
    expert_home = jax.random.permutation(key_of[4], EXPERTS).astype(jnp.int32)
    swap_flag = draw_swap_flag(jax.random.fold_in(key_of[8], 71), 0)
    weight_in = gaussian(key_of[6], (EXPERTS, D, F), D ** -0.5, 0.09375, ((0, 32), (1, 8)))
    weight_out = gaussian(key_of[7], (EXPERTS, F, D), F ** -0.5, 0.21875, ((0, 32), (2, 8)))
    return dict(tokens=tokens, cotangent=cotangent, expert_ids=expert_ids, gate_values=gate_values, expert_home=expert_home, swap_flag=swap_flag, weight_in=weight_in, weight_out=weight_out)


def regroup(array):
    shaped = array.reshape((N_EXPERT, N_DP, TOK_DEV) + array.shape[1:])
    return jnp.swapaxes(shaped, 0, 1).reshape((N_DP, N_EXPERT * TOK_DEV) + array.shape[1:])


def ungroup(array):
    shaped = array.reshape((N_DP, N_EXPERT, TOK_DEV) + array.shape[2:])
    return jnp.swapaxes(shaped, 0, 1).reshape((TOKENS,) + array.shape[2:])


def reference(tokens, cotangent, expert_ids, gate_values, expert_home, swap_flag, weight_in, weight_out):
    half_axis = EXPERTS // 2
    capacity_rows = EXPERTS * CAP
    group_x = regroup(tokens)
    group_cot = regroup(cotangent)
    group_slot = regroup(expert_home[expert_ids]).reshape(N_DP, -1)
    group_gate = regroup(gate_values).reshape(N_DP, -1)
    contract_rows = (((0,), (0,)), ((), ()))
    contract_cols = (((1,), (1,)), ((), ()))

    def per_slot(carry, slot_index):
        flagged = swap_flag[slot_index % half_axis]
        source = jnp.where(flagged == 1, (slot_index + half_axis) % EXPERTS, slot_index).astype(jnp.int32)
        mat_in = lax.dynamic_index_in_dim(weight_in, source, 0, keepdims=False)
        mat_out = lax.dynamic_index_in_dim(weight_out, source, 0, keepdims=False)

        def per_group(inputs):
            rows_x, rows_cot, slots, gates = inputs
            matches = slots == slot_index
            picked = jnp.nonzero(matches, size=capacity_rows, fill_value=0)[0].astype(jnp.int32)
            live_rows = jnp.arange(capacity_rows) < jnp.sum(matches)
            token_rows = picked // TOP
            routed_x = jnp.where(live_rows[:, None], rows_x[token_rows], 0).astype(jnp.bfloat16)
            scaled = gates[picked][:, None] * rows_cot[token_rows].astype(jnp.float32)
            routed_dy = jnp.where(live_rows[:, None], scaled, 0.0).astype(jnp.bfloat16)
            pre_act = jnp.dot(routed_x, mat_in, preferred_element_type=jnp.float32)
            hidden = jax.nn.silu(pre_act).astype(jnp.bfloat16)
            hidden_grad = lax.dot_general(routed_dy, mat_out, contract_cols, preferred_element_type=jnp.float32)
            sigmoid_a = jax.nn.sigmoid(pre_act)
            pre_grad = (hidden_grad * sigmoid_a * (1.0 + pre_act * (1.0 - sigmoid_a))).astype(jnp.bfloat16)
            pair_grad = lax.dot_general(pre_grad, mat_in, contract_cols, preferred_element_type=jnp.float32).astype(jnp.bfloat16)
            masked = jnp.where(live_rows[:, None], pair_grad.astype(jnp.float32), 0.0)
            token_grad = jnp.zeros(rows_x.shape, jnp.float32).at[token_rows].add(masked)
            part_in = lax.dot_general(routed_x, pre_grad, contract_rows, preferred_element_type=jnp.float32).astype(jnp.bfloat16)
            part_out = lax.dot_general(hidden, routed_dy, contract_rows, preferred_element_type=jnp.float32).astype(jnp.bfloat16)
            return token_grad, part_in, part_out

        token_grad, part_in, part_out = lax.map(per_group, (group_x, group_cot, group_slot, group_gate))
        slot_in = jnp.sum(part_in.astype(jnp.float32), axis=0).astype(jnp.bfloat16)
        slot_out = jnp.sum(part_out.astype(jnp.float32), axis=0).astype(jnp.bfloat16)
        return carry + token_grad, (slot_in, slot_out)

    start = jnp.zeros((N_DP, N_EXPERT * TOK_DEV, D), jnp.float32)
    total, (weight_in_grad, weight_out_grad) = lax.scan(per_slot, start, jnp.arange(EXPERTS, dtype=jnp.int32))
    grad_tokens = ungroup(total).astype(jnp.bfloat16)
    return (grad_tokens, weight_in_grad, weight_out_grad)
```

```python
import jax
import jax.numpy as jnp
from jax import lax
from jax.sharding import Mesh, PartitionSpec as P

AXES = ("y", "w", "core", "x", "p")
SIZES = (4, 4, 2, 4, 2)
TOP = 8
BF = jnp.bfloat16
F32 = jnp.float32


def shift(value, axis, steps):
    count = lax.axis_size(axis)
    return lax.ppermute(value, axis, [(s, (s + steps) % count) for s in range(count)])


def lookup(table, keys, width):
    matches = keys[..., None] == jnp.arange(width, dtype=jnp.int32)
    return jnp.sum(jnp.where(matches, table, 0), axis=-1)


def dot(a, b, ca, cb):
    return lax.dot_general(a, b, (((ca,), (cb,)), ((), ())), preferred_element_type=F32)


def to_relative(rows, x, p):
    count, width = rows.shape
    cut = rows.reshape(count, 4, 2, width // 8)
    cut = jnp.where(p == 1, cut[:, :, ::-1], cut)
    return jnp.roll(cut, -x, axis=1).reshape(count, width)


def to_absolute(rows, x, p):
    count, width = rows.shape
    cut = rows.reshape(count, 4, 2, width // 8)
    cut = jnp.where(p == 1, cut[:, :, ::-1], cut)
    return jnp.roll(cut, x, axis=1).reshape(count, width)


def gather_blocks(own):
    other = shift(own, "p", 1)
    right0, left0 = shift(own, "x", 1), shift(own, "x", -1)
    right1, left1 = shift(other, "x", 1), shift(other, "x", -1)
    far1, far0 = shift(right1, "x", 1), shift(left0, "x", -1)
    return own, other, left0, left1, far0, far1, right0, right1


def add(*terms):
    total = terms[0].astype(F32)
    for term in terms[1:]:
        total = total + term.astype(F32)
    return total.astype(BF)


def scatter_blocks(block):
    from_left = shift(block(4), "x", 1)
    from_right = shift(block(5), "x", -1)
    left1, right1 = shift(block(3), "x", 1), shift(add(block(7), from_right), "x", -1)
    left0, right0 = shift(add(block(2), from_left), "x", 1), shift(block(6), "x", -1)
    partner = shift(add(block(1), left1, right1), "p", 1)
    return add(block(0), left0, right0, partner)


def gather_rows(rows):
    half = rows.shape[0] // 2
    right, left = shift(rows, "w", 1), shift(rows, "w", -1)
    far1, far0 = shift(right[half:], "w", 1), shift(left[:half], "w", -1)
    mine = jnp.concatenate([rows, left, far0, far1, right], axis=0)
    return jnp.concatenate([mine, shift(mine, "core", 1)], axis=0)


def body(tokens, cotangent, expert_ids, gate_values, expert_home, swap_flag, weight_in, weight_out):
    y, w, core, x, p = (lax.axis_index(axis) for axis in AXES)
    experts = 32
    half = experts // 2
    tok = tokens.shape[0]
    width = tokens.shape[1]
    cap = tok * TOP * 9 // (8 * experts)
    own_shard = (y * 4 + w) * 2 + core

    rows_x = to_relative(tokens, x, p)
    rows_c = to_relative(cotangent, x, p)

    source = jnp.where(
        jnp.concatenate([swap_flag, swap_flag]) == 1,
        (jnp.arange(experts, dtype=jnp.int32) + half) % experts,
        jnp.arange(experts, dtype=jnp.int32),
    )
    shard = lookup(lookup(source, expert_home, experts), expert_ids, experts)
    meta = jnp.concatenate([shard.astype(F32), gate_values], axis=1)
    meta_own = jnp.stack([meta, shift(meta, "w", -1), shift(meta, "w", 2), shift(meta, "w", 1)])
    meta_all = jnp.concatenate([meta_own, shift(meta_own, "core", 1)], axis=0)
    shard_all = meta_all[..., :TOP].astype(jnp.int32)
    gate_all = meta_all[..., TOP:]

    blocks_in = gather_blocks(weight_in[0])
    all_x = gather_rows(rows_x)
    all_c = gather_rows(rows_c)
    blocks_out = gather_blocks(weight_out[0])

    picks, send_x, send_dy = [], [], []
    for d in range(4):
        dest = (((y + d) % 4) * 4 + w) * 2 + core
        hit = shard_all == dest
        match = jnp.any(hit, axis=2)
        gate = jnp.sum(jnp.where(hit, gate_all, 0.0), axis=2)
        counted = match.astype(jnp.int32)
        rank = jnp.cumsum(counted, axis=1) - counted
        place = jnp.arange(8, dtype=jnp.int32)[:, None] * cap + rank
        place = jnp.where(match, place, -1).reshape(1, 8 * tok)
        chosen = jnp.arange(8 * cap, dtype=jnp.int32)[:, None] == place
        row_gate = jnp.sum(jnp.where(chosen, gate.reshape(1, 8 * tok), 0.0), axis=1, keepdims=True)
        pick = chosen.astype(BF)
        picks.append(pick)
        send_x.append(dot(pick, all_x, 1, 0).astype(BF))
        send_dy.append((dot(pick, all_c, 1, 0) * row_gate).astype(BF))
    pick_all = jnp.concatenate(picks, axis=0)
    routed_x = jnp.concatenate([send_x[0]] + [shift(send_x[d], "y", d) for d in (1, 2, 3)], axis=0)
    routed_dy = jnp.concatenate([send_dy[0]] + [shift(send_dy[d], "y", d) for d in (1, 2, 3)], axis=0)

    full_in = jnp.concatenate(blocks_in, axis=0)
    pre_act = dot(routed_x, full_in, 1, 0)
    sigmoid_a = jax.nn.sigmoid(pre_act)
    hidden = (pre_act * sigmoid_a).astype(BF)
    part = width // 8

    def columns(rows, b):
        return rows[:, b * part : (b + 1) * part]

    grad_out = scatter_blocks(lambda b: dot(hidden, columns(routed_dy, b), 0, 0).astype(BF))

    hidden_grad = sum(dot(columns(routed_dy, b), blocks_out[b], 1, 1) for b in range(8))
    pre_grad = (hidden_grad * sigmoid_a * (1.0 + pre_act * (1.0 - sigmoid_a))).astype(BF)

    grad_in = scatter_blocks(lambda b: dot(columns(routed_x, b), pre_grad, 0, 0).astype(BF))

    group = 8 * cap
    returned = []
    for d in range(4):
        rows = dot(pre_grad[d * group : (d + 1) * group], full_in, 1, 1).astype(BF)
        returned.append(shift(rows, "y", -d) if d else rows)
    returned = jnp.concatenate(returned, axis=0)
    near = 4 * tok
    theirs = dot(pick_all[:, near:], returned, 0, 0).astype(BF)
    mine = add(dot(pick_all[:, :near], returned, 0, 0), shift(theirs, "core", 1))
    mine = mine.reshape(4, tok, width)
    mid = tok // 2
    from_left, from_right = shift(mine[2, :mid], "w", 1), shift(mine[2, mid:], "w", -1)
    to_right = jnp.concatenate([add(mine[1, :mid], from_left), mine[1, mid:]], axis=0)
    to_left = jnp.concatenate([mine[3, :mid], add(mine[3, mid:], from_right)], axis=0)
    token_grad = add(mine[0], shift(to_right, "w", 1), shift(to_left, "w", -1))
    token_grad = to_absolute(token_grad, x, p)

    flag = lookup(swap_flag, own_shard % half, half)
    grad_out = jnp.where(flag == 1, shift(grad_out, "y", 2), grad_out)
    grad_in = jnp.where(flag == 1, shift(grad_in, "y", 2), grad_in)
    return (token_grad, grad_in[None], grad_out[None])


def solution(mesh):
    cut = Mesh(mesh.devices.reshape(SIZES), AXES)
    expert, dp = AXES[:3], AXES[3:]
    in_specs = (
        P(AXES, None),
        P(AXES, None),
        P(AXES, None),
        P(AXES, None),
        P(),
        P(),
        P(expert, dp, None),
        P(expert, None, dp),
    )
    out_specs = (P(AXES, None), P(expert, dp, None), P(expert, None, dp))
    return jax.shard_map(body, mesh=cut, in_specs=in_specs, out_specs=out_specs, check_vma=False)
```

```python
import jax
import jax.numpy as jnp
from jax import lax
from jax.experimental import pallas as pl
from jax.experimental.pallas import tpu as pltpu
from jax.sharding import Mesh, PartitionSpec as P

AXES = ("y", "w", "core", "x", "p")
SIZES = (4, 4, 2, 4, 2)
EXPERTS = 32
TOP = 8
TOK = 48
CAP = TOK * TOP * 9 // (8 * EXPERTS)
NEAR = 8
GROUP = NEAR * CAP
SOURCE = NEAR * TOK
PAD = 128
BF = jnp.bfloat16
F32 = jnp.float32
I32 = jnp.int32
VMEM_LIMIT = 24 * 1024 * 1024


def shift(value, axis, steps):
    count = lax.axis_size(axis)
    return lax.ppermute(value, axis, [(s, (s + steps) % count) for s in range(count)])


def after(value, *others):
    return lax.optimization_barrier((value,) + others)[0]


def dot(a, b, ca, cb):
    return lax.dot_general(a, b, (((ca,), (cb,)), ((), ())), preferred_element_type=F32)


def add(*terms):
    total = terms[0].astype(F32)
    for term in terms[1:]:
        total = total + term.astype(F32)
    return total.astype(BF)


def block_offset(b, x, p, part):
    place = lax.rem(x + b // 2, 4) * 2 + (lax.rem(p + 1, 2) if b % 2 else p)
    return pl.multiple_of(place * part, part)


def iota(shape, axis):
    return lax.broadcasted_iota(I32, shape, axis)


def prepare_kernel(at, home, flag, tok, cot, ids, gate, w_in, w_out, out_x, out_c, out_w):
    x, p = at[3], at[4]
    width = tok.shape[1]
    part = width // 8
    for b in range(8):
        src = block_offset(b, x, p, part)
        out_x[:, b * part : (b + 1) * part] = tok[:, pl.ds(src, part)]
        out_c[:, b * part : (b + 1) * part] = cot[:, pl.ds(src, part)]
    names = ids[...]
    shard = jnp.zeros(names.shape, I32)
    half = EXPERTS // 2
    for e in range(EXPERTS):
        slot = home[e]
        swapped = flag[lax.rem(slot, half)] == 1
        holder = jnp.where(swapped, lax.rem(slot + half, EXPERTS), slot)
        shard = jnp.where(names == e, holder, shard)
    g = gate[...]
    high = g.astype(BF)
    rest = g - high.astype(F32)
    middle = rest.astype(BF)
    low = (rest - middle.astype(F32)).astype(BF)
    extra = jnp.zeros((tok.shape[0], PAD), F32)
    for j, piece in enumerate((shard.astype(F32).astype(BF), high, middle, low)):
        spot = (iota((TOP, PAD), 1) == iota((TOP, PAD), 0) + j * TOP).astype(BF)
        extra = extra + jnp.dot(piece, spot, preferred_element_type=F32)
    out_x[:, width:] = extra.astype(BF)
    out_c[:, width:] = extra.astype(BF)
    rows = w_in.shape[0]
    out_w[0:rows, :] = w_in[...]
    out_w[rows:, :] = w_out[...].T


def prepare(at, home, flag, tok, cot, ids, gate, w_in, w_out):
    smem = pl.BlockSpec(memory_space=pltpu.SMEM)
    vmem = pl.BlockSpec(memory_space=pltpu.VMEM)
    wide = jax.ShapeDtypeStruct((tok.shape[0], tok.shape[1] + PAD), BF)
    return pl.pallas_call(
        prepare_kernel,
        in_specs=[smem] * 3 + [vmem] * 6,
        out_specs=[vmem] * 3,
        out_shape=[wide, wide, jax.ShapeDtypeStruct((2 * w_in.shape[0], w_in.shape[1]), BF)],
        compiler_params=pltpu.CompilerParams(vmem_limit_bytes=VMEM_LIMIT),
    )(at, home, flag, tok, cot, ids, gate, w_in, w_out)


def blocks_of(shape):
    token = iota(shape, 0)
    return sum((token >= TOK * j).astype(I32) for j in range(1, NEAR))


def ranks(match):
    square = (SOURCE, SOURCE)
    row, col = iota(square, 0), iota(square, 1)
    row_block = sum((row >= TOK * j).astype(I32) for j in range(1, NEAR))
    col_block = sum((col >= TOK * j).astype(I32) for j in range(1, NEAR))
    earlier = ((row_block == col_block) & (col < row)).astype(F32).astype(BF)
    return jnp.dot(earlier, match.astype(BF), preferred_element_type=F32)


def one_hot_rows(place, d):
    across = place.T
    return (iota((PAD, SOURCE), 0).astype(F32) == across[d : d + 1, :]).astype(F32).astype(BF)


def dispatch_kernel(at, near, far, near_meta, far_meta, s0, s1, s2, s3, spread, pick, scale):
    y, w, core = at[0], at[1], at[2]

    @pl.when(pl.program_id(0) == 0)
    def _():
        meta = jnp.concatenate([near_meta[...], far_meta[...]], axis=0).astype(F32)
        lane = iota((SOURCE, PAD), 1)
        widen_row, widen_col = iota((PAD, PAD), 0), iota((PAD, PAD), 1)
        widen = sum((widen_col == widen_row + TOP * j).astype(F32) for j in (1, 2, 3)).astype(BF)
        match = jnp.zeros((SOURCE, PAD), F32)
        weight = []
        for d in range(4):
            dest = (lax.rem(y + d, 4) * 4 + w) * 2 + core
            hit = jnp.where((meta == dest.astype(F32)) & (lane < TOP), 1.0, 0.0)
            match = jnp.where(lane == d, jnp.sum(hit, axis=1, keepdims=True), match)
            parts = jnp.dot(hit.astype(BF), widen, preferred_element_type=F32) * meta
            weight.append(parts.astype(BF))
        rank = ranks(match)
        place = jnp.where(match > 0.0, blocks_of((SOURCE, PAD)).astype(F32) * CAP + rank, -1.0)
        for d in range(4):
            chosen = one_hot_rows(place, d)
            pick[d * PAD : (d + 1) * PAD, :] = chosen
            parts = jnp.dot(chosen, weight[d], preferred_element_type=F32)
            scale[d * PAD : (d + 1) * PAD, :] = jnp.broadcast_to(
                jnp.sum(parts, axis=1, keepdims=True), (PAD, PAD)
            )
        for j in range(NEAR):
            other = lax.rem(core + j // 4, 2)
            target = pl.multiple_of((lax.rem(w + j % 4, 4) * 2 + other) * TOK, TOK)
            here = place[j * TOK : (j + 1) * TOK, :]
            for d in range(4):
                hits = iota((TOK, PAD), 1).astype(F32) == here[:, d : d + 1]
                spread[pl.ds(target, TOK), d * PAD : (d + 1) * PAD] = hits.astype(F32).astype(BF)

    rows = jnp.concatenate([near[...], far[...]], axis=0)
    for d, out in enumerate((s0, s1, s2, s3)):
        chosen = jnp.dot(pick[d * PAD : (d + 1) * PAD, :], rows, preferred_element_type=F32)
        chosen = chosen * scale[d * PAD : (d + 1) * PAD, 0:1]
        out[...] = chosen[:GROUP].astype(BF)


def dispatch(at, near, far, width):
    part = width // 8
    rows = pl.BlockSpec((NEAR // 2 * TOK, part), lambda i: (0, i))
    meta = pl.BlockSpec((NEAR // 2 * TOK, PAD), lambda i: (0, width // PAD))
    return pl.pallas_call(
        dispatch_kernel,
        grid=(8,),
        in_specs=[pl.BlockSpec(memory_space=pltpu.SMEM), rows, rows, meta, meta],
        out_specs=[pl.BlockSpec((GROUP, part), lambda i: (0, i))] * 4
        + [pl.BlockSpec((SOURCE, 4 * PAD), lambda i: (0, 0))],
        out_shape=[jax.ShapeDtypeStruct((GROUP, width), BF)] * 4
        + [jax.ShapeDtypeStruct((SOURCE, 4 * PAD), BF)],
        scratch_shapes=[pltpu.VMEM((4 * PAD, SOURCE), BF), pltpu.VMEM((4 * PAD, PAD), F32)],
        compiler_params=pltpu.CompilerParams(vmem_limit_bytes=VMEM_LIMIT),
    )(at, near, far, near, far)


def collect_kernel(at, rows, meta, out, pick):
    y, w, core = at[0], at[1], at[2]
    own = (y * 4 + w) * 2 + core

    def rows_from(d):
        return pl.ds(pl.multiple_of(lax.rem(y + 4 - d, 4) * SOURCE, SOURCE), SOURCE)

    @pl.when(pl.program_id(0) == 0)
    def _():
        lane = iota((SOURCE, PAD), 1)
        match = jnp.zeros((SOURCE, PAD), F32)
        for d in range(4):
            here = meta[rows_from(d), :].astype(F32)
            hit = jnp.where((here == own.astype(F32)) & (lane < TOP), 1.0, 0.0)
            match = jnp.where(lane == d, jnp.sum(hit, axis=1, keepdims=True), match)
        rank = ranks(match)
        block = blocks_of((SOURCE, PAD))
        order = jnp.zeros((SOURCE, PAD), I32)
        for j in range(NEAR):
            relative = lax.rem(core + j % 2, 2) * 4 + lax.rem(j // 2 + 4 - w, 4)
            order = jnp.where(block == j, relative, order)
        place = jnp.where(match > 0.0, order.astype(F32) * CAP + rank, -1.0)
        for d in range(4):
            pick[d * PAD : (d + 1) * PAD, :] = one_hot_rows(place, d)

    chosen = [
        jnp.dot(pick[d * PAD : (d + 1) * PAD, :], rows[rows_from(d), :], preferred_element_type=F32)
        for d in range(4)
    ]
    out[...] = jnp.concatenate([c[:GROUP] for c in chosen], axis=0).astype(BF)


def collect(at, every, width):
    part = width // 8
    return pl.pallas_call(
        collect_kernel,
        grid=(8,),
        in_specs=[
            pl.BlockSpec(memory_space=pltpu.SMEM),
            pl.BlockSpec((4 * SOURCE, part), lambda i: (0, i)),
            pl.BlockSpec((4 * SOURCE, PAD), lambda i: (0, width // PAD)),
        ],
        out_specs=pl.BlockSpec((4 * GROUP, part), lambda i: (0, i)),
        out_shape=jax.ShapeDtypeStruct((4 * GROUP, width), BF),
        scratch_shapes=[pltpu.VMEM((4 * PAD, SOURCE), BF)],
        compiler_params=pltpu.CompilerParams(vmem_limit_bytes=VMEM_LIMIT),
    )(at, every, every)


def restore_kernel(at, rows, out):
    x, p = at[3], at[4]
    part = rows.shape[1] // 8
    for b in range(8):
        out[:, pl.ds(block_offset(b, x, p, part), part)] = rows[:, b * part : (b + 1) * part]


def restore(at, rows):
    vmem = pl.BlockSpec(memory_space=pltpu.VMEM)
    return pl.pallas_call(
        restore_kernel,
        in_specs=[pl.BlockSpec(memory_space=pltpu.SMEM), vmem],
        out_specs=vmem,
        out_shape=jax.ShapeDtypeStruct(rows.shape, BF),
        compiler_params=pltpu.CompilerParams(vmem_limit_bytes=VMEM_LIMIT),
    )(at, rows)


def gather_weights(own):
    half = own.shape[0] // 2
    right0, left0 = shift(own, "x", 1), shift(own, "x", -1)
    other = shift(own, "p", 1)
    far0_in, far0_out = shift(left0[:half], "x", -1), shift(right0[half:], "x", 1)
    ready = after(other, right0, left0)
    right1, left1 = shift(ready, "x", 1), shift(ready, "x", -1)
    far1_in, far1_out = shift(left1[:half], "x", -1), shift(right1[half:], "x", 1)
    whole = {0: own, 1: other, 2: left0, 3: left1, 6: right0, 7: right1}
    ins = {b: v[:half] for b, v in whole.items()} | {4: far0_in, 5: far1_in}
    outs = {b: v[half:] for b, v in whole.items()} | {4: far0_out, 5: far1_out}
    return [ins[b] for b in range(8)], [outs[b] for b in range(8)]


def scatter_blocks(block):
    from_left = shift(block(4), "x", 1)
    from_right = shift(block(5), "x", -1)
    left1, right1 = shift(block(3), "x", 1), shift(add(block(7), from_right), "x", -1)
    left0, right0 = shift(add(block(2), from_left), "x", 1), shift(block(6), "x", -1)
    partner = shift(add(block(1), left1, right1), "p", 1)
    return add(block(0), left0, right0, partner)


def gather_near(rows):
    half = (rows.shape[1] // PAD + 1) // 2 * PAD
    right, left = shift(rows, "w", 1), shift(rows, "w", -1)
    far0, far1 = shift(left[:, :half], "w", -1), shift(right[:, half:], "w", 1)
    far = jnp.concatenate([far0, far1], axis=1)
    mine = jnp.concatenate([rows, left, far, right], axis=0)
    return mine, shift(mine, "core", 1)


def body(tokens, cotangent, expert_ids, gate_values, expert_home, swap_flag, weight_in, weight_out):
    at = jnp.stack([lax.axis_index(axis) for axis in AXES]).astype(I32)
    width = tokens.shape[1]
    part = width // 8

    rows_x, rows_c, weights = prepare(
        at, expert_home, swap_flag, tokens, cotangent, expert_ids, gate_values, weight_in[0], weight_out[0]
    )
    every_x = lax.all_gather(rows_x, AXES[:3], axis=0, tiled=True)
    in_blocks, out_blocks = gather_weights(weights)
    near, far = gather_near(rows_c)
    *send, spread = dispatch(at, near, far, width)
    spread = spread.reshape(SOURCE, 4, PAD)[:, :, :GROUP].reshape(SOURCE, 4 * GROUP)
    routed_dy = jnp.concatenate([send[0]] + [shift(send[d], "y", d) for d in (1, 2, 3)], axis=0)
    routed_x = collect(at, every_x, width)

    def columns(rows, b):
        return rows[:, b * part : (b + 1) * part]

    pre_act = sum(dot(columns(routed_x, b), in_blocks[b], 1, 0) for b in range(8))
    sigmoid_a = jax.nn.sigmoid(pre_act)
    hidden = (pre_act * sigmoid_a).astype(BF)
    grad_out = scatter_blocks(lambda b: dot(hidden, columns(routed_dy, b), 0, 0).astype(BF))

    hidden_grad = sum(dot(columns(routed_dy, b), out_blocks[b], 1, 0) for b in range(8))
    pre_grad = (hidden_grad * sigmoid_a * (1.0 + pre_act * (1.0 - sigmoid_a))).astype(BF)
    grad_in = scatter_blocks(lambda b: dot(columns(routed_x, b), pre_grad, 0, 0).astype(BF))

    full_in = jnp.concatenate(in_blocks, axis=0)
    returned = []
    for d in range(4):
        rows = dot(pre_grad[d * GROUP : (d + 1) * GROUP], full_in, 1, 1).astype(BF)
        returned.append(shift(rows, "y", -d) if d else rows)
    by_device = dot(spread, jnp.concatenate(returned, axis=0), 1, 0).astype(BF)
    token_grad = lax.psum_scatter(by_device, AXES[1:3], scatter_dimension=0, tiled=True)
    token_grad = restore(at, token_grad)

    half = EXPERTS // 2
    pair = lax.rem((at[0] * 4 + at[1]) * 2 + at[2], half)
    flag = jnp.sum(jnp.where(jnp.arange(half, dtype=I32) == pair, swap_flag, 0))
    grad_out = jnp.where(flag == 1, shift(grad_out, "y", 2), grad_out)
    grad_in = jnp.where(flag == 1, shift(grad_in, "y", 2), grad_in)
    return (token_grad, grad_in[None], grad_out[None])


def solution(mesh):
    cut = Mesh(mesh.devices.reshape(SIZES), AXES)
    expert, dp = AXES[:3], AXES[3:]
    in_specs = (
        P(AXES, None),
        P(AXES, None),
        P(AXES, None),
        P(AXES, None),
        P(),
        P(),
        P(expert, dp, None),
        P(expert, None, dp),
    )
    out_specs = (P(AXES, None), P(expert, dp, None), P(expert, None, dp))
    return jax.shard_map(body, mesh=cut, in_specs=in_specs, out_specs=out_specs, check_vma=False)
```

```python
import jax
import jax.numpy as jnp
from jax import lax
from jax.experimental import pallas as pl
from jax.experimental.pallas import tpu as pltpu
from jax.sharding import Mesh, PartitionSpec as P

AXES = ("y", "w", "core", "x", "p")
SIZES = (4, 4, 2, 4, 2)
EXPERTS = 32
TOP = 8
TOK = 48
CAP = TOK * TOP * 9 // (8 * EXPERTS)
NEAR = 8
GROUP = NEAR * CAP
SOURCE = NEAR * TOK
PAD = 128
BF = jnp.bfloat16
F32 = jnp.float32
I32 = jnp.int32
VMEM_LIMIT = 24 * 1024 * 1024


def shift(value, axis, steps):
    count = lax.axis_size(axis)
    return lax.ppermute(value, axis, [(s, (s + steps) % count) for s in range(count)])


def after(value, *others):
    return lax.optimization_barrier((value,) + others)[0]


def dot(a, b, ca, cb):
    return lax.dot_general(a, b, (((ca,), (cb,)), ((), ())), preferred_element_type=F32)


def add(*terms):
    total = terms[0].astype(F32)
    for term in terms[1:]:
        total = total + term.astype(F32)
    return total.astype(BF)


def block_offset(b, x, p, part):
    place = lax.rem(x + b // 2, 4) * 2 + (lax.rem(p + 1, 2) if b % 2 else p)
    return pl.multiple_of(place * part, part)


def iota(shape, axis):
    return lax.broadcasted_iota(I32, shape, axis)


def prepare_kernel(at, home, tok, cot, ids, gate, out_x, out_c):
    x, p = at[3], at[4]
    width = tok.shape[1]
    part = width // 8
    for b in range(8):
        src = block_offset(b, x, p, part)
        out_x[:, b * part : (b + 1) * part] = tok[:, pl.ds(src, part)]
        out_c[:, b * part : (b + 1) * part] = cot[:, pl.ds(src, part)]
    names = ids[...]
    shard = jnp.zeros(names.shape, I32)
    for e in range(EXPERTS):
        shard = jnp.where(names == e, home[e], shard)
    g = gate[...]
    high = g.astype(BF)
    rest = g - high.astype(F32)
    middle = rest.astype(BF)
    low = (rest - middle.astype(F32)).astype(BF)
    extra = jnp.zeros((tok.shape[0], PAD), F32)
    for j, piece in enumerate((shard.astype(F32).astype(BF), high, middle, low)):
        spot = (iota((TOP, PAD), 1) == iota((TOP, PAD), 0) + j * TOP).astype(BF)
        extra = extra + jnp.dot(piece, spot, preferred_element_type=F32)
    out_x[:, width:] = extra.astype(BF)


def prepare(at, home, tok, cot, ids, gate):
    smem = pl.BlockSpec(memory_space=pltpu.SMEM)
    vmem = pl.BlockSpec(memory_space=pltpu.VMEM)
    wide = jax.ShapeDtypeStruct((tok.shape[0], tok.shape[1] + PAD), BF)
    return pl.pallas_call(
        prepare_kernel,
        in_specs=[smem] * 2 + [vmem] * 4,
        out_specs=[vmem] * 2,
        out_shape=[wide, jax.ShapeDtypeStruct(cot.shape, BF)],
        compiler_params=pltpu.CompilerParams(vmem_limit_bytes=VMEM_LIMIT),
    )(at, home, tok, cot, ids, gate)


def turn_kernel(flag, own, far, out):
    out[...] = jnp.where(flag[0] == 1, far[...], own[...]).T


def turn(flag, own, far):
    vmem = pl.BlockSpec(memory_space=pltpu.VMEM)
    return pl.pallas_call(
        turn_kernel,
        in_specs=[pl.BlockSpec(memory_space=pltpu.SMEM), vmem, vmem],
        out_specs=vmem,
        out_shape=jax.ShapeDtypeStruct(own.shape[::-1], BF),
        compiler_params=pltpu.CompilerParams(vmem_limit_bytes=VMEM_LIMIT),
    )(flag.reshape(1), own, far)


def blocks_of(shape):
    token = iota(shape, 0)
    return sum((token >= TOK * j).astype(I32) for j in range(1, NEAR))


def ranks(match):
    square = (SOURCE, SOURCE)
    row, col = iota(square, 0), iota(square, 1)
    row_block = sum((row >= TOK * j).astype(I32) for j in range(1, NEAR))
    col_block = sum((col >= TOK * j).astype(I32) for j in range(1, NEAR))
    earlier = ((row_block == col_block) & (col < row)).astype(F32).astype(BF)
    return jnp.dot(earlier, match.astype(BF), preferred_element_type=F32)


def cut_rows(pick, rows, outs, scale=None):
    for d, out in enumerate(outs):
        chosen = jnp.dot(pick[d * PAD : (d + 1) * PAD, :], rows, preferred_element_type=F32)
        if scale is not None:
            chosen = chosen * scale[d * PAD : (d + 1) * PAD, 0:1]
        out[...] = chosen[:GROUP].astype(BF)


def select_kernel(at, rows, meta_ref, s0, s1, s2, s3, spread, pick, scale, places):
    y, w, core = at[0], at[1], at[2]

    @pl.when(pl.program_id(0) == 0)
    def _():
        meta = meta_ref[...].astype(F32)
        lane = iota((SOURCE, PAD), 1)
        widen_row, widen_col = iota((PAD, PAD), 0), iota((PAD, PAD), 1)
        widen = sum((widen_col == widen_row + TOP * j).astype(F32) for j in (1, 2, 3)).astype(BF)
        match = jnp.zeros((SOURCE, PAD), F32)
        weight = []
        for d in range(4):
            dest = (lax.rem(y + d, 4) * 4 + w) * 2 + core
            hit = jnp.where((meta == dest.astype(F32)) & (lane < TOP), 1.0, 0.0)
            match = jnp.where(lane == d, jnp.sum(hit, axis=1, keepdims=True), match)
            parts = jnp.dot(hit.astype(BF), widen, preferred_element_type=F32) * meta
            weight.append(parts.astype(BF))
        rank = ranks(match)
        place = jnp.where(match > 0.0, blocks_of((SOURCE, PAD)).astype(F32) * CAP + rank, -1.0)
        across = place.T
        for d in range(4):
            chosen = (iota((PAD, SOURCE), 0).astype(F32) == across[d : d + 1, :]).astype(F32).astype(BF)
            pick[d * PAD : (d + 1) * PAD, :] = chosen
            parts = jnp.dot(chosen, weight[d], preferred_element_type=F32)
            scale[d * PAD : (d + 1) * PAD, :] = jnp.broadcast_to(
                jnp.sum(parts, axis=1, keepdims=True), (PAD, PAD)
            )
        places[...] = place
        for j in range(NEAR):
            device = lax.rem(w + j % 4, 4) * 2 + lax.rem(core + j // 4, 2)
            here = places[pl.ds(pl.multiple_of(device * TOK, TOK), TOK), :]
            for d in range(4):
                hits = iota((TOK, PAD), 1).astype(F32) == here[:, d : d + 1]
                spread[j * TOK : (j + 1) * TOK, d * PAD : (d + 1) * PAD] = hits.astype(F32).astype(BF)

    cut_rows(pick, rows[...], (s0, s1, s2, s3))


def select(at, every, width):
    part = width // 8
    still = lambda i: (0, 0)
    return pl.pallas_call(
        select_kernel,
        grid=(8,),
        in_specs=[
            pl.BlockSpec(memory_space=pltpu.SMEM),
            pl.BlockSpec((SOURCE, part), lambda i: (0, i)),
            pl.BlockSpec((SOURCE, PAD), lambda i: (0, width // PAD)),
        ],
        out_specs=[pl.BlockSpec((GROUP, part), lambda i: (0, i))] * 4
        + [
            pl.BlockSpec((SOURCE, 4 * PAD), still),
            pl.BlockSpec((4 * PAD, SOURCE), still),
            pl.BlockSpec((4 * PAD, PAD), still),
        ],
        out_shape=[jax.ShapeDtypeStruct((GROUP, width), BF)] * 4
        + [
            jax.ShapeDtypeStruct((SOURCE, 4 * PAD), BF),
            jax.ShapeDtypeStruct((4 * PAD, SOURCE), BF),
            jax.ShapeDtypeStruct((4 * PAD, PAD), F32),
        ],
        scratch_shapes=[pltpu.VMEM((SOURCE, PAD), F32)],
        compiler_params=pltpu.CompilerParams(vmem_limit_bytes=VMEM_LIMIT),
    )(at, every, every)


def weigh_kernel(rows, pick, scale, *outs):
    cut_rows(pick, rows[...], outs, scale)


def weigh(every, pick, scale, width):
    part = width // 8
    return pl.pallas_call(
        weigh_kernel,
        grid=(8,),
        in_specs=[
            pl.BlockSpec((SOURCE, part), lambda i: (0, i)),
            pl.BlockSpec(pick.shape, lambda i: (0, 0)),
            pl.BlockSpec(scale.shape, lambda i: (0, 0)),
        ],
        out_specs=[pl.BlockSpec((GROUP, part), lambda i: (0, i))] * 4,
        out_shape=[jax.ShapeDtypeStruct((GROUP, width), BF)] * 4,
        compiler_params=pltpu.CompilerParams(vmem_limit_bytes=VMEM_LIMIT),
    )(every, pick, scale)


def restore_kernel(at, one, two, three, out):
    x, p = at[3], at[4]
    part = one.shape[1] // 8
    for b in range(8):
        here = slice(b * part, (b + 1) * part)
        total = one[:, here].astype(F32) + two[:, here].astype(F32) + three[:, here].astype(F32)
        out[:, pl.ds(block_offset(b, x, p, part), part)] = total.astype(BF)


def restore(at, one, two, three):
    vmem = pl.BlockSpec(memory_space=pltpu.VMEM)
    return pl.pallas_call(
        restore_kernel,
        in_specs=[pl.BlockSpec(memory_space=pltpu.SMEM)] + [vmem] * 3,
        out_specs=vmem,
        out_shape=jax.ShapeDtypeStruct(one.shape, BF),
        compiler_params=pltpu.CompilerParams(vmem_limit_bytes=VMEM_LIMIT),
    )(at, one, two, three)


def ring():
    last = []

    def step(to_right, to_left, *others):
        if last or others:
            to_right = after(to_right, *last[:1], *others)
            to_left = after(to_left, *last[1:], *others)
        last[:] = shift(to_right, "x", 1), shift(to_left, "x", -1)
        return tuple(last)

    return step


def pair_kernel(pre, *refs):
    blocks, outs = refs[:8], refs[8:]
    part = blocks[0].shape[0]
    rows = pre[...]
    for b in range(8):
        grad = dot(rows, blocks[b][...], 1, 1)
        for d in range(4):
            outs[d][:, b * part : (b + 1) * part] = grad[d * GROUP : (d + 1) * GROUP].astype(BF)


def pair_gradients(pre_grad, blocks):
    vmem = pl.BlockSpec(memory_space=pltpu.VMEM)
    return pl.pallas_call(
        pair_kernel,
        in_specs=[vmem] * 9,
        out_specs=[vmem] * 4,
        out_shape=[jax.ShapeDtypeStruct((GROUP, 8 * blocks[0].shape[0]), BF)] * 4,
        compiler_params=pltpu.CompilerParams(vmem_limit_bytes=VMEM_LIMIT),
    )(pre_grad, *blocks)


def body(tokens, cotangent, expert_ids, gate_values, expert_home, swap_flag, weight_in, weight_out):
    at = jnp.stack([lax.axis_index(axis) for axis in AXES]).astype(I32)
    width = tokens.shape[1]
    part = width // 8

    half = EXPERTS // 2
    pair = lax.rem((at[0] * 4 + at[1]) * 2 + at[2], half)
    flag = jnp.sum(jnp.where(jnp.arange(half, dtype=I32) == pair, swap_flag, 0))
    paired_in = shift(weight_in[0], "y", 2)
    paired_out = shift(after(weight_out[0], paired_in), "y", 2)
    own_in = jnp.where(flag == 1, paired_in, weight_in[0])
    own_out = turn(flag, weight_out[0], paired_out)

    rows_x, rows_c = prepare(at, expert_home, tokens, cotangent, expert_ids, gate_values)
    near_x = lax.all_gather(rows_x, AXES[1:3], axis=0, tiled=True)
    other_in = shift(own_in, "p", 1)
    cut = own_out.shape[0] // 2
    upper = shift(after(own_out[:cut], other_in), "p", 1)
    other_out = jnp.concatenate([upper, shift(after(own_out[cut:], upper), "p", 1)], axis=0)
    ins, outs = {0: own_in, 1: other_in}, {0: own_out, 1: other_out}

    step = ring()
    ins[6], ins[2] = step(own_in, own_in)
    outs[6], outs[2] = step(own_out, own_out)
    near_c = lax.all_gather(after(rows_c, near_x, ins[6], ins[2]), AXES[1:3], axis=0, tiled=True)
    *send_x, spread, pick, scale = select(at, after(near_x, ins[6], ins[2], other_in), width)
    spread = spread.reshape(SOURCE, 4, PAD)[:, :, :GROUP].reshape(SOURCE, 4 * GROUP)
    ins[7], ins[3] = step(other_in, other_in, near_x)
    x1, x3 = shift(send_x[1], "y", 1), shift(send_x[3], "y", 3)
    ins[5], ins[4] = step(ins[7], ins[2], x1, x3)
    x2 = shift(after(send_x[2], x1, x3, ins[7], ins[3]), "y", 2)
    send_dy = weigh(after(near_c, ins[5], ins[4]), pick, scale, width)
    outs[7], outs[3] = step(other_out, other_out, x2, *send_dy)
    x1, x2, x3 = after((x1, x2, x3), *send_dy)
    routed_x = jnp.concatenate([send_x[0], x1, x2, x3], axis=0)
    dy1, dy3 = shift(send_dy[1], "y", 1), shift(send_dy[3], "y", 3)
    outs[5], outs[4] = step(outs[7], outs[2], dy1, dy3)
    dy2 = shift(after(send_dy[2], dy1, dy3), "y", 2)
    routed_dy = jnp.concatenate([send_dy[0], dy1, dy2, dy3], axis=0)

    def columns(rows, b):
        return rows[:, b * part : (b + 1) * part]

    pre_act = sum(dot(columns(routed_x, b), ins[b], 1, 0) for b in range(8))
    sigmoid_a = jax.nn.sigmoid(pre_act)
    hidden = (pre_act * sigmoid_a).astype(BF)
    hidden_grad = sum(dot(columns(routed_dy, b), outs[b], 1, 0) for b in (0, 1, 2, 3, 6, 7, 4, 5))
    pre_grad = (hidden_grad * sigmoid_a * (1.0 + pre_act * (1.0 - sigmoid_a))).astype(BF)

    def term_in(b):
        return dot(columns(routed_x, b), pre_grad, 0, 0).astype(BF)

    def term_out(b):
        return dot(hidden, columns(routed_dy, b), 0, 0).astype(BF)

    step = ring()
    out_far = step(term_out(4), term_out(5))
    back = pair_gradients(pre_grad, [ins[b] for b in range(8)])
    back1, back3 = shift(back[1], "y", -1), shift(back[3], "y", -3)
    in_far = step(term_in(4), term_in(5))
    back2 = shift(after(back[2], back1, back3), "y", -2)
    out_one = step(term_out(3), add(term_out(7), out_far[1]), back1, back3)
    returned = jnp.concatenate([back[0], back1, back2, back3], axis=0)
    near = SOURCE // 2
    theirs = dot(spread[near:], returned, 1, 0).astype(BF)
    in_one = step(term_in(3), add(term_in(7), in_far[1]), theirs)
    mine = add(dot(spread[:near], returned, 1, 0), shift(theirs, "core", 1)).reshape(4, TOK, width)
    out_other = shift(add(term_out(1), *out_one), "p", 1)
    mid = width // 2
    far_right, far_left = shift(mine[2, :, :mid], "w", 1), shift(mine[2, :, mid:], "w", -1)
    out_zero = step(add(term_out(2), out_far[0]), term_out(6), far_right, far_left)
    to_right = jnp.concatenate([add(mine[1, :, :mid], far_right), mine[1, :, mid:]], axis=1)
    to_left = jnp.concatenate([mine[3, :, :mid], add(mine[3, :, mid:], far_left)], axis=1)
    from_left, from_right = shift(to_right, "w", 1), shift(to_left, "w", -1)
    in_other = shift(add(term_in(1), *in_one), "p", 1)
    in_zero = step(add(term_in(2), in_far[0]), term_in(6), out_other)
    grad_out = add(term_out(0), *out_zero, out_other)
    grad_in = add(term_in(0), *in_zero, in_other)
    token_grad = restore(at, mine[0], from_left, from_right)
    return (token_grad, grad_in[None], grad_out[None])


def solution(mesh):
    cut = Mesh(mesh.devices.reshape(SIZES), AXES)
    expert, dp = AXES[:3], AXES[3:]
    in_specs = (
        P(AXES, None),
        P(AXES, None),
        P(AXES, None),
        P(AXES, None),
        P(),
        P(),
        P(expert, dp, None),
        P(expert, None, dp),
    )
    out_specs = (P(AXES, None), P(expert, dp, None), P(expert, None, dp))
    return jax.shard_map(body, mesh=cut, in_specs=in_specs, out_specs=out_specs, check_vma=False)
```

```python
import jax
import jax.numpy as jnp
from jax import lax
from jax.experimental import pallas as pl
from jax.experimental.pallas import tpu as pltpu
from jax.sharding import Mesh, PartitionSpec as P

AXES = ("y", "w", "core", "x", "p")
SIZES = (4, 4, 2, 4, 2)
EXPERTS = 32
TOP = 8
TOK = 48
CAP = TOK * TOP * 9 // (8 * EXPERTS)
NEAR = 8
GROUP = NEAR * CAP
SOURCE = NEAR * TOK
PAD = 128
BF = jnp.bfloat16
F32 = jnp.float32
I32 = jnp.int32
VMEM_LIMIT = 24 * 1024 * 1024


def shift(value, axis, steps):
    count = lax.axis_size(axis)
    return lax.ppermute(value, axis, [(s, (s + steps) % count) for s in range(count)])


def after(value, *others):
    return lax.optimization_barrier((value,) + others)[0]


def dot(a, b, ca, cb):
    return lax.dot_general(a, b, (((ca,), (cb,)), ((), ())), preferred_element_type=F32)


def add(*terms):
    total = terms[0].astype(F32)
    for term in terms[1:]:
        total = total + term.astype(F32)
    return total.astype(BF)


def block_offset(b, x, p, part):
    place = lax.rem(x + b // 2, 4) * 2 + (lax.rem(p + 1, 2) if b % 2 else p)
    return pl.multiple_of(place * part, part)


def iota(shape, axis):
    return lax.broadcasted_iota(I32, shape, axis)


def prepare_kernel(at, home, tok, cot, ids, gate, out_x, out_c):
    x, p = at[3], at[4]
    width = tok.shape[1]
    part = width // 8
    for b in range(8):
        src = block_offset(b, x, p, part)
        out_x[:, b * part : (b + 1) * part] = tok[:, pl.ds(src, part)]
        out_c[:, b * part : (b + 1) * part] = cot[:, pl.ds(src, part)]
    names = ids[...]
    shard = jnp.zeros(names.shape, I32)
    for e in range(EXPERTS):
        shard = jnp.where(names == e, home[e], shard)
    g = gate[...]
    high = g.astype(BF)
    rest = g - high.astype(F32)
    middle = rest.astype(BF)
    low = (rest - middle.astype(F32)).astype(BF)
    extra = jnp.zeros((tok.shape[0], PAD), F32)
    for j, piece in enumerate((shard.astype(F32).astype(BF), high, middle, low)):
        spot = (iota((TOP, PAD), 1) == iota((TOP, PAD), 0) + j * TOP).astype(BF)
        extra = extra + jnp.dot(piece, spot, preferred_element_type=F32)
    out_x[:, width:] = extra.astype(BF)


def prepare(at, home, tok, cot, ids, gate):
    smem = pl.BlockSpec(memory_space=pltpu.SMEM)
    vmem = pl.BlockSpec(memory_space=pltpu.VMEM)
    wide = jax.ShapeDtypeStruct((tok.shape[0], tok.shape[1] + PAD), BF)
    return pl.pallas_call(
        prepare_kernel,
        in_specs=[smem] * 2 + [vmem] * 4,
        out_specs=[vmem] * 2,
        out_shape=[wide, jax.ShapeDtypeStruct(cot.shape, BF)],
        compiler_params=pltpu.CompilerParams(vmem_limit_bytes=VMEM_LIMIT),
    )(at, home, tok, cot, ids, gate)


def turn_kernel(flag, own, far, out):
    out[...] = jnp.where(flag[0] == 1, far[...], own[...]).T


def turn(flag, own, far):
    vmem = pl.BlockSpec(memory_space=pltpu.VMEM)
    return pl.pallas_call(
        turn_kernel,
        in_specs=[pl.BlockSpec(memory_space=pltpu.SMEM), vmem, vmem],
        out_specs=vmem,
        out_shape=jax.ShapeDtypeStruct(own.shape[::-1], BF),
        compiler_params=pltpu.CompilerParams(vmem_limit_bytes=VMEM_LIMIT),
    )(flag.reshape(1), own, far)


def blocks_of(shape):
    token = iota(shape, 0)
    return sum((token >= TOK * j).astype(I32) for j in range(1, NEAR))


def ranks(match):
    square = (SOURCE, SOURCE)
    row, col = iota(square, 0), iota(square, 1)
    row_block = sum((row >= TOK * j).astype(I32) for j in range(1, NEAR))
    col_block = sum((col >= TOK * j).astype(I32) for j in range(1, NEAR))
    earlier = ((row_block == col_block) & (col < row)).astype(F32).astype(BF)
    return jnp.dot(earlier, match.astype(BF), preferred_element_type=F32)


def cut_rows(pick, rows, outs, scale=None):
    for d, out in enumerate(outs):
        chosen = jnp.dot(pick[d * PAD : (d + 1) * PAD, :], rows, preferred_element_type=F32)
        if scale is not None:
            chosen = chosen * scale[d * PAD : (d + 1) * PAD, 0:1]
        out[...] = chosen[:GROUP].astype(BF)


def select_kernel(at, rows, meta_ref, s0, s1, s2, s3, spread, pick, scale, places):
    y, w, core = at[0], at[1], at[2]

    @pl.when(pl.program_id(0) == 0)
    def _():
        meta = meta_ref[...].astype(F32)
        lane = iota((SOURCE, PAD), 1)
        widen_row, widen_col = iota((PAD, PAD), 0), iota((PAD, PAD), 1)
        widen = sum((widen_col == widen_row + TOP * j).astype(F32) for j in (1, 2, 3)).astype(BF)
        match = jnp.zeros((SOURCE, PAD), F32)
        weight = []
        for d in range(4):
            dest = (lax.rem(y + d, 4) * 4 + w) * 2 + core
            hit = jnp.where((meta == dest.astype(F32)) & (lane < TOP), 1.0, 0.0)
            match = jnp.where(lane == d, jnp.sum(hit, axis=1, keepdims=True), match)
            parts = jnp.dot(hit.astype(BF), widen, preferred_element_type=F32) * meta
            weight.append(parts.astype(BF))
        rank = ranks(match)
        place = jnp.where(match > 0.0, blocks_of((SOURCE, PAD)).astype(F32) * CAP + rank, -1000.0)
        across = place.T
        for d in range(4):
            chosen = (iota((PAD, SOURCE), 0).astype(F32) == across[d : d + 1, :]).astype(F32).astype(BF)
            pick[d * PAD : (d + 1) * PAD, :] = chosen
            parts = jnp.dot(chosen, weight[d], preferred_element_type=F32)
            scale[d * PAD : (d + 1) * PAD, :] = jnp.broadcast_to(
                jnp.sum(parts, axis=1, keepdims=True), (PAD, PAD)
            )
        places[...] = place
        for j in range(NEAR):
            device = lax.rem(w + j % 4, 4) * 2 + lax.rem(core + j // 4, 2)
            here = places[pl.ds(pl.multiple_of(device * TOK, TOK), TOK), :]
            row = iota((TOK, 4 * GROUP), 1).astype(F32)
            hits = [row == here[:, d : d + 1] + float(d * GROUP) for d in range(4)]
            taken = sum(h.astype(F32) for h in hits)
            spread[j * TOK : (j + 1) * TOK, :] = taken.astype(BF)

    cut_rows(pick, rows[...], (s0, s1, s2, s3))


def select(at, every, width):
    part = width // 8
    still = lambda i: (0, 0)
    return pl.pallas_call(
        select_kernel,
        grid=(8,),
        in_specs=[
            pl.BlockSpec(memory_space=pltpu.SMEM),
            pl.BlockSpec((SOURCE, part), lambda i: (0, i)),
            pl.BlockSpec((SOURCE, PAD), lambda i: (0, width // PAD)),
        ],
        out_specs=[pl.BlockSpec((GROUP, part), lambda i: (0, i))] * 4
        + [
            pl.BlockSpec((SOURCE, 4 * GROUP), still),
            pl.BlockSpec((4 * PAD, SOURCE), still),
            pl.BlockSpec((4 * PAD, PAD), still),
        ],
        out_shape=[jax.ShapeDtypeStruct((GROUP, width), BF)] * 4
        + [
            jax.ShapeDtypeStruct((SOURCE, 4 * GROUP), BF),
            jax.ShapeDtypeStruct((4 * PAD, SOURCE), BF),
            jax.ShapeDtypeStruct((4 * PAD, PAD), F32),
        ],
        scratch_shapes=[pltpu.VMEM((SOURCE, PAD), F32)],
        compiler_params=pltpu.CompilerParams(vmem_limit_bytes=VMEM_LIMIT),
    )(at, every, every)


def weigh_kernel(rows, pick, scale, *outs):
    cut_rows(pick, rows[...], outs, scale)


def weigh(every, pick, scale, width):
    part = width // 8
    return pl.pallas_call(
        weigh_kernel,
        grid=(8,),
        in_specs=[
            pl.BlockSpec((SOURCE, part), lambda i: (0, i)),
            pl.BlockSpec(pick.shape, lambda i: (0, 0)),
            pl.BlockSpec(scale.shape, lambda i: (0, 0)),
        ],
        out_specs=[pl.BlockSpec((GROUP, part), lambda i: (0, i))] * 4,
        out_shape=[jax.ShapeDtypeStruct((GROUP, width), BF)] * 4,
        compiler_params=pltpu.CompilerParams(vmem_limit_bytes=VMEM_LIMIT),
    )(every, pick, scale)


def restore_kernel(at, one, two, three, out):
    x, p = at[3], at[4]
    part = one.shape[1] // 8
    for b in range(8):
        here = slice(b * part, (b + 1) * part)
        total = one[:, here].astype(F32) + two[:, here].astype(F32) + three[:, here].astype(F32)
        out[:, pl.ds(block_offset(b, x, p, part), part)] = total.astype(BF)


def restore(at, one, two, three):
    vmem = pl.BlockSpec(memory_space=pltpu.VMEM)
    return pl.pallas_call(
        restore_kernel,
        in_specs=[pl.BlockSpec(memory_space=pltpu.SMEM)] + [vmem] * 3,
        out_specs=vmem,
        out_shape=jax.ShapeDtypeStruct(one.shape, BF),
        compiler_params=pltpu.CompilerParams(vmem_limit_bytes=VMEM_LIMIT),
    )(at, one, two, three)


def ring():
    last = []

    def step(to_right, to_left, *others):
        if last or others:
            to_right = after(to_right, *last[:1], *others)
            to_left = after(to_left, *last[1:], *others)
        last[:] = shift(to_right, "x", 1), shift(to_left, "x", -1)
        return tuple(last)

    return step


def pair_kernel(pre, *refs):
    blocks, outs = refs[:8], refs[8:]
    part = blocks[0].shape[0]
    rows = pre[...]
    for b in range(8):
        grad = dot(rows, blocks[b][...], 1, 1)
        for d in range(4):
            outs[d][:, b * part : (b + 1) * part] = grad[d * GROUP : (d + 1) * GROUP].astype(BF)


def pair_gradients(pre_grad, blocks):
    vmem = pl.BlockSpec(memory_space=pltpu.VMEM)
    return pl.pallas_call(
        pair_kernel,
        in_specs=[vmem] * 9,
        out_specs=[vmem] * 4,
        out_shape=[jax.ShapeDtypeStruct((GROUP, 8 * blocks[0].shape[0]), BF)] * 4,
        compiler_params=pltpu.CompilerParams(vmem_limit_bytes=VMEM_LIMIT),
    )(pre_grad, *blocks)


def body(tokens, cotangent, expert_ids, gate_values, expert_home, swap_flag, weight_in, weight_out):
    at = jnp.stack([lax.axis_index(axis) for axis in AXES]).astype(I32)
    width = tokens.shape[1]
    part = width // 8

    half = EXPERTS // 2
    pair = lax.rem((at[0] * 4 + at[1]) * 2 + at[2], half)
    flag = jnp.sum(jnp.where(jnp.arange(half, dtype=I32) == pair, swap_flag, 0))
    paired_in = shift(weight_in[0], "y", 2)
    paired_out = shift(after(weight_out[0], paired_in), "y", 2)
    own_in = jnp.where(flag == 1, paired_in, weight_in[0])
    own_out = turn(flag, weight_out[0], paired_out)

    rows_x, rows_c = prepare(at, expert_home, tokens, cotangent, expert_ids, gate_values)
    near_x = lax.all_gather(rows_x, AXES[1:3], axis=0, tiled=True)
    cut = own_in.shape[0] // 2
    in_upper = shift(own_in[:cut], "p", 1)
    in_lower = shift(after(own_in[cut:], in_upper), "p", 1)
    other_in = jnp.concatenate([in_upper, in_lower], axis=0)
    other_out = shift(after(own_out, in_lower), "p", 1)
    ins, outs = {0: own_in, 1: other_in}, {0: own_out, 1: other_out}

    step = ring()
    ins[6], ins[2] = step(own_in, own_in)
    outs[6], outs[2] = step(own_out, own_out)
    near_c = lax.all_gather(after(rows_c, near_x, ins[6], ins[2], own_out, in_upper), AXES[1:3], axis=0, tiled=True)
    *send_x, spread, pick, scale = select(at, after(near_x, ins[6], ins[2]), width)
    ins[7], ins[3] = step(other_in, other_in, near_x)
    x1, x3 = shift(send_x[1], "y", 1), shift(send_x[3], "y", 3)
    ins[5], ins[4] = step(ins[7], ins[2], x1, x3)
    x2 = shift(after(send_x[2], x1, x3, ins[7], ins[3]), "y", 2)
    send_dy = weigh(after(near_c, ins[7], ins[3]), pick, scale, width)
    outs[7], outs[3] = step(other_out, other_out, x2, *send_dy)
    x1, x2, x3 = after((x1, x2, x3), *send_dy)
    routed_x = jnp.concatenate([send_x[0], x1, x2, x3], axis=0)
    dy1, dy3 = shift(send_dy[1], "y", 1), shift(send_dy[3], "y", 3)
    outs[5], outs[4] = step(outs[7], outs[2], dy1, dy3)
    dy2 = shift(after(send_dy[2], dy1, dy3), "y", 2)
    routed_dy = jnp.concatenate([send_dy[0], dy1, dy2, dy3], axis=0)

    def columns(rows, b):
        return rows[:, b * part : (b + 1) * part]

    pre_act = sum(dot(columns(routed_x, b), ins[b], 1, 0) for b in range(8))
    sigmoid_a = jax.nn.sigmoid(pre_act)
    hidden = (pre_act * sigmoid_a).astype(BF)
    hidden_grad = sum(dot(columns(routed_dy, b), outs[b], 1, 0) for b in (0, 1, 2, 3, 6, 7, 4, 5))
    pre_grad = (hidden_grad * sigmoid_a * (1.0 + pre_act * (1.0 - sigmoid_a))).astype(BF)

    def term_in(b):
        return dot(columns(routed_x, b), pre_grad, 0, 0).astype(BF)

    def term_out(b):
        return dot(hidden, columns(routed_dy, b), 0, 0).astype(BF)

    step = ring()
    out_far = step(term_out(4), term_out(5))
    back = pair_gradients(pre_grad, [ins[b] for b in range(8)])
    back = after(tuple(back), *out_far)
    back1, back3 = shift(back[1], "y", -1), shift(back[3], "y", -3)
    in_far = step(term_in(4), term_in(5))
    back2 = shift(after(back[2], back1, back3), "y", -2)
    out_one = step(term_out(3), add(term_out(7), out_far[1]), back1, back3)
    returned = jnp.concatenate([back[0], back1, back2, back3], axis=0)
    returned = after(returned, *out_one)
    near = SOURCE // 2
    theirs = dot(spread[near:], returned, 1, 0).astype(BF)
    in_one = step(term_in(3), add(term_in(7), in_far[1]), back2)
    mine = add(dot(spread[:near], returned, 1, 0), shift(theirs, "core", 1)).reshape(4, TOK, width)
    out_other = shift(add(term_out(1), *out_one), "p", 1)
    mid = width // 2
    far_right, far_left = shift(mine[2, :, :mid], "w", 1), shift(mine[2, :, mid:], "w", -1)
    out_zero = step(add(term_out(2), out_far[0]), term_out(6), mine)
    to_right = jnp.concatenate([add(mine[1, :, :mid], far_right), mine[1, :, mid:]], axis=1)
    to_left = jnp.concatenate([mine[3, :, :mid], add(mine[3, :, mid:], far_left)], axis=1)
    from_left, from_right = shift(to_right, "w", 1), shift(to_left, "w", -1)
    in_other = shift(add(term_in(1), *in_one), "p", 1)
    in_zero = step(add(term_in(2), in_far[0]), term_in(6), out_other, far_right, far_left)
    grad_out = add(term_out(0), *out_zero, out_other)
    grad_in = add(term_in(0), *in_zero, in_other)
    token_grad = restore(at, mine[0], from_left, from_right)
    return (token_grad, grad_in[None], grad_out[None])


def solution(mesh):
    cut = Mesh(mesh.devices.reshape(SIZES), AXES)
    expert, dp = AXES[:3], AXES[3:]
    in_specs = (
        P(AXES, None),
        P(AXES, None),
        P(AXES, None),
        P(AXES, None),
        P(),
        P(),
        P(expert, dp, None),
        P(expert, None, dp),
    )
    out_specs = (P(AXES, None), P(expert, dp, None), P(expert, None, dp))
    return jax.shard_map(body, mesh=cut, in_specs=in_specs, out_specs=out_specs, check_vma=False)
```
